256 devices in a mesh: ctx: 64 (over z, y_hi, x), head: 4 (over y_lo, core).
Axes of the slice: x: 4, y: 4 (y_hi: 2, y_lo: 2; y = y_hi * 2 + y_lo), z: 8, core: 2. Of those that a mesh axis runs over, the one named last changes fastest.
Arguments:
- lin_query: bfloat16 [24576, 8192], P('ctx', 'head'), may hold values from -600 to 600
- lin_key: bfloat16 [24576, 8192], P('ctx', 'head'), may hold values from -6 to 6
- lin_value: bfloat16 [24576, 8192], P('ctx', 'head'), may hold values from -6 to 6
- log_decay: float32 [64, 24576], P('head', 'ctx'), may hold values from -1 to 0
- soft_query: bfloat16 [24576, 8192], P('ctx', 'head'), may hold values from -300 to 300
- soft_key: bfloat16 [24576, 8192], P('ctx', 'head'), may hold values from -6 to 6
- soft_value: bfloat16 [24576, 8192], P('ctx', 'head'), may hold values from -6 to 6
Outputs:
- linear_out: bfloat16 [24576, 8192], P('ctx', 'head')
- window_out: bfloat16 [24576, 8192], P('ctx', 'head')
The draws below stay inside these ranges and needn't reach their ends.
All inputs are finite; a program needn't handle non-finite values.
Results may differ from the reference program's by a relative error of at most 0.011.
Values may be sent and summed in bfloat16 or wider, within the bound.
A program may use at most 192 MiB of HBM per device.

```python
import math
import jax
import jax.numpy as jnp
from jax import lax

HEADS = 64
DH = 128
TOK_DEV = 384
CONTEXT_LENGTH = 24576
WIN = 768


def draw_log_decay(key, part):
    key = jax.random.fold_in(key, 11)
    prng_seed_pool = jax.random.split(key, 6)
    switch_count = HEADS // 2
    blocks_count = CONTEXT_LENGTH // TOK_DEV
    head_order = jax.random.permutation(prng_seed_pool[0], HEADS)
    switching = (head_order < switch_count)[:, None, None]
    quick_blocks = jax.random.uniform(prng_seed_pool[5], (HEADS, blocks_count, 1)) < 0.5
    quick_tiles = jnp.logical_and(switching, quick_blocks)
    quick_tiles = jnp.broadcast_to(quick_tiles, (HEADS, blocks_count, TOK_DEV)).reshape(HEADS, CONTEXT_LENGTH)
    pace_rate = jnp.where(quick_tiles, 1.0 / 40.0, 1.0 / CONTEXT_LENGTH)
    tile_multiplier = jnp.exp(jax.random.uniform(prng_seed_pool[1], (HEADS, blocks_count, 1), minval=-0.7, maxval=0.7))
    tile_multiplier = jnp.broadcast_to(tile_multiplier, (HEADS, blocks_count, TOK_DEV)).reshape(HEADS, CONTEXT_LENGTH)
    seed_shift_amount = jax.random.uniform(prng_seed_pool[2], (HEADS, CONTEXT_LENGTH), minval=0.5, maxval=1.5)
    packet_bundles = jax.random.uniform(prng_seed_pool[3], (1, CONTEXT_LENGTH)) < 4.0 / CONTEXT_LENGTH
    layer_tiers = jnp.log(jax.random.uniform(prng_seed_pool[4], (1, CONTEXT_LENGTH), minval=0.5, maxval=0.8))
    return -pace_rate * tile_multiplier * seed_shift_amount + jnp.where(packet_bundles, layer_tiers, 0.0)


def draw_lin_query(key, part):
    key = jax.random.fold_in(key, 12)
    prng_seed_pool = jax.random.split(key, 3)
    entries = jax.random.truncated_normal(prng_seed_pool[0], -6.0, 6.0, (CONTEXT_LENGTH, HEADS * DH))
    climb = 3.0
    head_rise = climb ** (jnp.arange(HEADS, dtype=jnp.float32) / max(HEADS - 1, 1))
    column_scale = jnp.repeat(head_rise, DH) * jnp.exp(jax.random.uniform(prng_seed_pool[1], (HEADS * DH,), minval=0.0, maxval=math.log(3.3)))
    row_scale = jnp.exp(jax.random.uniform(prng_seed_pool[2], (CONTEXT_LENGTH, 1), minval=0.0, maxval=math.log(10.0)))
    return (entries * column_scale[None, :] * row_scale).astype(jnp.bfloat16)


def drawn_parts(key):
    prng_seed_pool = jax.random.split(jax.random.fold_in(key, 70), 2)
    base_query = jax.random.truncated_normal(prng_seed_pool[0], -6.0, 6.0, (CONTEXT_LENGTH, HEADS * DH))
    base_key = jax.random.truncated_normal(prng_seed_pool[1], -6.0, 6.0, (CONTEXT_LENGTH, HEADS * DH))
    return (base_query, base_key)


def draw_soft_key(key, part):
    base_query, base_key = drawn_parts(key)
    return base_key.astype(jnp.bfloat16)


def draw_soft_query(key, part):
    base_query, base_key = drawn_parts(key)
    return base_query.astype(jnp.bfloat16)


def block_scale(stream_key, dims, shards, least, largest):
    factor_of, own = 1.0, jax.random.fold_in(stream_key, 6)
    for axis_at, blocks in shards:
        steps = jnp.exp(jax.random.uniform(jax.random.fold_in(own, axis_at), (blocks,), jnp.float32, least / len(shards), largest / len(shards)))
        factor_of = factor_of * jnp.repeat(steps, dims[axis_at] // blocks).reshape([-1 if axis == axis_at else 1 for axis in range(len(dims))])
    return factor_of


def scatter_about(rng, shape, width, bound, pieces=(), kind=jnp.bfloat16):
    values = jax.random.normal(rng, shape, jnp.float32) * width
    if len(pieces) > 0:
        values = block_scale(rng, shape, pieces, -0.22, 0.18) * values
    return jnp.clip(values, min=-bound, max=bound).astype(kind)


def setup_inputs(seed: int = 0) -> dict:
    arg_keys = jax.random.split(jax.random.key(seed), 8)
    lin_query = draw_lin_query(jax.random.fold_in(arg_keys[7], 71), 0)
    lin_key = scatter_about(arg_keys[1], (CONTEXT_LENGTH, HEADS * DH), 1.0, 6.0, ((0, 64), (1, 4)))
    lin_value = scatter_about(arg_keys[2], (CONTEXT_LENGTH, HEADS * DH), 1.0, 6.0, ((0, 64), (1, 4)))
    log_decay = draw_log_decay(jax.random.fold_in(arg_keys[7], 71), 0)
    soft_query = draw_soft_query(jax.random.fold_in(arg_keys[7], 71), 0)
    soft_key = draw_soft_key(jax.random.fold_in(arg_keys[7], 71), 0)
    soft_value = scatter_about(arg_keys[6], (CONTEXT_LENGTH, HEADS * DH), 1.0, 6.0, ((0, 64), (1, 4)))
    return dict(lin_query=lin_query, lin_key=lin_key, lin_value=lin_value, log_decay=log_decay, soft_query=soft_query, soft_key=soft_key, soft_value=soft_value)


def lightning_layer(lin_query, lin_key, lin_value, log_decay):
    blocks_count = CONTEXT_LENGTH // TOK_DEV
    q_blocks = lin_query.reshape(blocks_count, TOK_DEV, HEADS, DH)
    k_blocks = lin_key.reshape(blocks_count, TOK_DEV, HEADS, DH)
    v_blocks = lin_value.reshape(blocks_count, TOK_DEV, HEADS, DH)
    d_blocks = log_decay.reshape(HEADS, blocks_count, TOK_DEV).transpose(1, 0, 2)
    positions = jnp.arange(TOK_DEV, dtype=jnp.int32)
    causal = positions[:, None] >= positions[None, :]

    def advance(prefix, block_data):
        q_blk, k_blk, v_blk, d_blk = block_data
        cumulative = jnp.cumsum(d_blk, axis=1)
        block_total = cumulative[:, -1]
        decay_mask = jnp.exp(jnp.where(causal[None], cumulative[:, :, None] - cumulative[:, None, :], -jnp.inf))
        q_wide = q_blk.astype(jnp.float32)
        v_wide = v_blk.astype(jnp.float32)
        scores = jnp.einsum('thd,shd->hts', q_wide, k_blk.astype(jnp.float32))
        weights = (scores * decay_mask).astype(jnp.bfloat16)
        inside_part = jnp.einsum('hts,shd->thd', weights.astype(jnp.float32), v_wide)
        carried_part = jnp.einsum('thd,hde->the', q_wide, prefix, precision=lax.Precision.HIGHEST)
        combined = inside_part + carried_part * jnp.exp(cumulative).T[:, :, None]
        mean_sq = lax.optimization_barrier(jnp.mean(combined * combined, axis=(1, 2), keepdims=True))
        normed = (combined * lax.rsqrt(mean_sq + 1e-05)).astype(jnp.bfloat16).reshape(TOK_DEV, HEADS * DH)
        decayed = (k_blk.astype(jnp.float32) * jnp.exp(block_total[:, None] - cumulative).T[:, :, None]).astype(jnp.bfloat16)
        local_state = jnp.einsum('shd,she->hde', decayed.astype(jnp.float32), v_wide)
        return (jnp.exp(block_total)[:, None, None] * prefix + local_state, normed)
    start_state = jnp.zeros((HEADS, DH, DH), jnp.float32)
    final_state, outputs = lax.scan(advance, start_state, (q_blocks, k_blocks, v_blocks, d_blocks))
    return outputs.reshape(CONTEXT_LENGTH, HEADS * DH)

def window_layer(window_query, soft_key, window_value):
    front_zeros = jnp.zeros((2 * TOK_DEV, HEADS * DH), jnp.bfloat16)
    key_pad = jnp.concatenate([front_zeros, soft_key], axis=0)
    value_pad = jnp.concatenate([front_zeros, window_value], axis=0)

    def window_block(block_index):
        row_start = (block_index * TOK_DEV).astype(jnp.int32)
        q_blk = lax.dynamic_slice_in_dim(window_query, row_start, TOK_DEV, 0).reshape(TOK_DEV, HEADS, DH).astype(jnp.float32)
        k_blk = lax.dynamic_slice_in_dim(key_pad, row_start, 3 * TOK_DEV, 0).reshape(3 * TOK_DEV, HEADS, DH).astype(jnp.float32)
        v_blk = lax.dynamic_slice_in_dim(value_pad, row_start, 3 * TOK_DEV, 0).reshape(3 * TOK_DEV, HEADS, DH).astype(jnp.float32)
        scores = jnp.einsum('thd,shd->hts', q_blk, k_blk) * DH ** (-0.5)
        q_pos = block_index * TOK_DEV + jnp.arange(TOK_DEV, dtype=jnp.int32)
        k_pos = (block_index - 2) * TOK_DEV + jnp.arange(3 * TOK_DEV, dtype=jnp.int32)
        allowed = (k_pos[None, :] >= 0) & (k_pos[None, :] <= q_pos[:, None]) & (q_pos[:, None] - k_pos[None, :] <= WIN)
        scores = jnp.where(allowed[None], scores, -jnp.inf)
        row_max = lax.optimization_barrier(jnp.max(scores, axis=-1, keepdims=True))
        raised = jnp.exp(scores - row_max)
        probability = (raised / lax.optimization_barrier(jnp.sum(raised, axis=-1, keepdims=True))).astype(jnp.bfloat16)
        result = jnp.einsum('hts,shd->thd', probability.astype(jnp.float32), v_blk)
        return result.astype(jnp.bfloat16).reshape(TOK_DEV, HEADS * DH)
    outputs = lax.map(window_block, jnp.arange(CONTEXT_LENGTH // TOK_DEV, dtype=jnp.int32))
    return outputs.reshape(CONTEXT_LENGTH, HEADS * DH)

def reference(lin_query, lin_key, lin_value, log_decay, soft_query, soft_key, soft_value):
    linear_out = lightning_layer(lin_query, lin_key, lin_value, log_decay)
    linear_wide = linear_out.astype(jnp.float32)
    window_query = (soft_query.astype(jnp.float32) + linear_wide).astype(jnp.bfloat16)
    window_value = (soft_value.astype(jnp.float32) + linear_wide).astype(jnp.bfloat16)
    window_out = window_layer(window_query, soft_key, window_value)
    return (linear_out, window_out)
```

```python
import jax
import jax.numpy as jnp
from jax import lax
from jax.experimental import pallas as pl
from jax.experimental.pallas import tpu as pltpu
from jax.sharding import PartitionSpec as P

MESH = pl.DeviceIdType.MESH
F32, BF16 = jnp.float32, jnp.bfloat16
DH = 128
H = 16
TOK = 384
NX = 4
NR = 16
NHEAD = 4
G = H // NX
WIN = 768
LINE = NX * TOK
SPAN = WIN + LINE
QT = 128
KT = WIN + QT
EARLY = (True, True, False, False)
LOG2E = 1.4426950408889634


def nt(a, b, **kw):
    return lax.dot_general(a, b, (((1,), (1,)), ((), ())), preferred_element_type=F32, **kw)


def tn(a, b):
    return lax.dot_general(a, b, (((0,), (0,)), ((), ())), preferred_element_type=F32)


def nn(a, b):
    return jnp.dot(a, b, preferred_element_type=F32)


def kernel(
    lq, lk, lv, ld, sq, sk, sv, lin_out, win_out,
    vq, vk, vv, lsq, lsv, lout, cumrow, colb, inside, acc,
    tot, totx, rowtot, rowtots, st, sx, tsrc, trows, pout, prow, px, pre,
    sqs, sqr, kb, vb, qb, lb, ob,
    load, tsem, rtsem, ssem, trsem, psem, xsem, qsem,
    ksem, khsem, vhsem, aqsem, avsem, losem, osem, osend,
):
    c = lax.axis_index("ctx")
    h = lax.axis_index("head")
    r, x = lax.div(c, NX), lax.rem(c, NX)

    def line(k):
        return lax.rem(x + k, NX)

    def row(k):
        return lax.rem(r + k, NR)

    def xdev(k):
        return (r * NX + line(k), h)

    def rdev(k):
        return (row(k) * NX + x, h)

    def hdev(k):
        return (c, lax.rem(h + k, NHEAD))

    def remote(src, dst, sems, dev):
        pltpu.make_async_remote_copy(
            src_ref=src, dst_ref=dst, send_sem=sems.at[0], recv_sem=sems.at[1],
            device_id=dev, device_id_type=MESH,
        ).start()

    def local(src, dst, sem):
        pltpu.make_async_copy(src, dst, sem).start()

    def drain(ref, sem):
        pltpu.make_async_copy(ref, ref, sem).wait()

    def cols(head):
        return pl.ds(pl.multiple_of(head * DH, DH), DH)

    def at_line(k, base=0):
        return pl.ds(pl.multiple_of(base + k * TOK, TOK), TOK)

    barrier = pltpu.get_barrier_semaphore()
    for k in range(1, NX):
        pl.semaphore_signal(barrier, inc=1, device_id=xdev(k), device_id_type=MESH)
    for k in range(1, NHEAD):
        pl.semaphore_signal(barrier, inc=1, device_id=hdev(k), device_id_type=MESH)

    def greet(k, carry):
        pl.semaphore_signal(barrier, inc=1, device_id=rdev(k), device_id_type=MESH)
        return carry

    lax.fori_loop(1, NR, greet, 0)

    local(lk, vk, load.at[0])
    local(lv, vv, load.at[1])
    local(lq, vq, load.at[2])
    for j in range(G):
        own = cols(x * G + j)
        local(sk.at[:, own], kb.at[j, at_line(x, WIN)], load.at[3])
        if EARLY[j]:
            local(sq.at[:, own], qb.at[j, at_line(x)], load.at[4])
            local(sv.at[:, own], vb.at[j, at_line(x, WIN)], load.at[4])
    if not all(EARLY):
        local(sq, lsq, load.at[5])
        local(sv, lsv, load.at[6])

    decay = ld[...]
    at_row = lax.broadcasted_iota(jnp.int32, (TOK, TOK), 0)
    at_col = lax.broadcasted_iota(jnp.int32, (TOK, TOK), 1)
    lower = jnp.where(at_row >= at_col, 1.0, 0.0).astype(F32)
    cumrow[...] = nt(decay, lower, precision=lax.Precision.HIGHEST)
    cum_col = nt(lower, decay, precision=lax.Precision.HIGHEST)
    for hh in range(H):
        colb[hh] = jnp.broadcast_to(cum_col[:, hh : hh + 1], (TOK, DH))
    tot[...] = jnp.broadcast_to(jnp.sum(decay, axis=1, keepdims=True), (H, DH))
    totx[x] = tot[...]

    pl.semaphore_wait(barrier, (NX - 1) + (NHEAD - 1) + (NR - 1))
    for k in range(1, NX):
        remote(tot, totx.at[x], tsem, xdev(k))

    def send_keys(j):
        for k in range(1, NX):
            remote(
                sk.at[:, cols(line(k) * G + j)], kb.at[j, at_line(x, WIN)], ksem.at[j], xdev(k)
            )

    send_keys(0)

    drain(vk, load.at[0])
    drain(vv, load.at[1])

    def state(hh, carry):
        k = vk[:, cols(hh)].astype(F32)
        fall = jnp.exp(tot[pl.ds(hh, 1), :] - colb[hh])
        st[hh] = tn((k * fall).astype(BF16), vv[:, cols(hh)]).astype(BF16)
        return carry

    for k in (2, 1, 3, 0):
        first = line(k) * G
        lax.fori_loop(first, first + G, state, 0)
        if k:
            remote(st.at[pl.ds(first, G)], sx.at[x], ssem, xdev(k))
    sx[x] = st[pl.ds(x * G, G)]

    drain(totx.at[pl.ds(0, NX - 1)], tsem.at[1])
    rowtot[...] = totx[0] + totx[1] + totx[2] + totx[3]
    rowtots[r] = rowtot[...]

    def send_rowtot(k, carry):
        remote(rowtot, rowtots.at[r], rtsem, rdev(k))
        return carry

    lax.fori_loop(1, NR, send_rowtot, 0)

    drain(vq, load.at[2])
    tri = lax.broadcasted_iota(jnp.int32, (QT, QT), 0) >= lax.broadcasted_iota(
        jnp.int32, (QT, QT), 1
    )

    def intra(hh, carry):
        q, k, v = vq[:, cols(hh)], vk[:, cols(hh)], vv[:, cols(hh)]
        crow = cumrow[pl.ds(hh, 1), :]
        for i in range(TOK // QT):
            n = (i + 1) * QT
            scores = nt(q[i * QT : n], k[:n])
            cc = colb[hh, i * QT : n, :]
            parts = []
            for s in range(i + 1):
                gap = cc - crow[:, s * QT : (s + 1) * QT]
                if s == i:
                    gap = jnp.where(tri, gap, -jnp.inf)
                parts.append((scores[:, s * QT : (s + 1) * QT] * jnp.exp(gap)).astype(BF16))
            weights = jnp.concatenate(parts, axis=1) if i else parts[0]
            inside[hh, i * QT : n, :] = nn(weights, v[:n])
        colb[hh] = jnp.exp(colb[hh])
        return carry

    lax.fori_loop(0, H, intra, 0)

    drain(sx.at[pl.ds(0, NX - 1)], ssem.at[1])

    def line_sum(g, carry):
        total = jnp.zeros((DH, DH), F32)
        for s in range(NX):
            total = jnp.exp(totx[s, pl.ds(x * G + g, 1), :]) * total + sx[s, g].astype(F32)
        tsrc[pl.ds(g * 4, 4)] = total.astype(BF16).reshape(4, DH // 4, DH)
        return carry

    lax.fori_loop(0, G, line_sum, 0)
    trows[r] = tsrc[r]

    def send_sum(k, carry):
        remote(tsrc.at[row(k)], trows.at[r], trsem, rdev(k))
        return carry

    lax.fori_loop(1, NR, send_sum, 0)
    for j in range(1, G):
        send_keys(j)

    drain(rowtots.at[pl.ds(0, NR - 1)], rtsem.at[1])
    drain(trows.at[pl.ds(0, NR - 1)], trsem.at[1])
    mine = x * G + lax.div(r, 4)

    def scan_rows(k, before):
        pout[k] = before.astype(BF16)
        return jnp.exp(rowtots[k, pl.ds(mine, 1), :]) * before + trows[k].astype(F32)

    lax.fori_loop(0, NR, scan_rows, jnp.zeros((DH // 4, DH), F32))
    prow[r] = pout[r]

    def send_before(k, carry):
        remote(pout.at[row(k)], prow.at[r], psem, rdev(k))
        return carry

    lax.fori_loop(1, NR, send_before, 0)
    drain(prow.at[pl.ds(0, NR - 1)], psem.at[1])

    def line_scan(g, carry):
        before = prow[pl.ds(g * 4, 4)].reshape(DH, DH).astype(F32)
        for s in range(NX):
            px[s, g] = before.astype(BF16)
            before = jnp.exp(totx[s, pl.ds(x * G + g, 1), :]) * before + sx[s, g].astype(F32)
        return carry

    lax.fori_loop(0, G, line_scan, 0)
    for k in (2, 1, 3):
        remote(px.at[line(k)], pre.at[pl.ds(x * G, G)], xsem, xdev(k))
    pre[pl.ds(x * G, G)] = px[x]

    for j in range(G):
        if EARLY[j]:
            for k in range(1, NX):
                other = cols(line(k) * G + j)
                remote(sv.at[:, other], vb.at[j, at_line(x, WIN)], avsem.at[j], xdev(k))
                remote(sq.at[:, other], qb.at[j, at_line(x)], aqsem.at[j], xdev(k))

    drain(kb.at[pl.ds(0, G), pl.ds(0, TOK)], load.at[3])
    for j in range(G):
        drain(kb.at[j, pl.ds(0, (NX - 1) * TOK)], ksem.at[j, 1])
        remote(kb.at[j, pl.ds(LINE, WIN)], kb.at[j, pl.ds(0, WIN)], khsem.at[j], rdev(1))

    acc[...] = jnp.zeros_like(acc)
    drain(pre.at[pl.ds(0, (NX - 1) * G)], xsem.at[1])

    def carry_in(hh, carry):
        both = inside[hh] + nn(vq[:, cols(hh)], pre[hh]) * colb[hh]
        inside[hh] = both
        acc[...] += both * both
        return carry

    lax.fori_loop(0, H, carry_in, 0)
    eye = at_row == at_col
    squares = jnp.sum(acc[...], axis=1, keepdims=True)
    as_row = jnp.sum(jnp.where(eye, squares, 0.0), axis=0, keepdims=True)
    sqs[...] = jnp.broadcast_to(as_row, sqs.shape)
    for k in range(1, NHEAD):
        remote(sqs, sqr.at[h], qsem, hdev(k))
    sqr[h] = sqs[...]
    if not all(EARLY):
        drain(lsq, load.at[5])
        drain(lsv, load.at[6])
    drain(sqr.at[pl.ds(0, NHEAD - 1)], qsem.at[1])
    feature_sum = sqr[0] + sqr[1] + sqr[2] + sqr[3]
    inverse = lax.rsqrt(feature_sum / (NHEAD * H * DH) + 1e-05)[0:1, :]
    as_col = jnp.sum(jnp.where(eye, inverse, 0.0), axis=1, keepdims=True)
    acc[...] = jnp.broadcast_to(as_col, acc.shape)

    for j in range(G):

        def normalize(k, carry):
            at = cols(k * G + j)
            out = (inside[k * G + j] * acc[...]).astype(BF16)
            lout[:, at] = out
            if not EARLY[j]:
                wide = out.astype(F32)
                lsq[:, at] = (lsq[:, at].astype(F32) + wide).astype(BF16)
                lsv[:, at] = (lsv[:, at].astype(F32) + wide).astype(BF16)
            return carry

        lax.fori_loop(0, NX, normalize, 0)
        for k in range(1, NX):
            other = cols(line(k) * G + j)
            if EARLY[j]:
                remote(lout.at[:, other], lb.at[j, at_line(x)], losem.at[j], xdev(k))
            else:
                remote(lsv.at[:, other], vb.at[j, at_line(x, WIN)], avsem.at[j], xdev(k))
                remote(lsq.at[:, other], qb.at[j, at_line(x)], aqsem.at[j], xdev(k))
        own = cols(x * G + j)
        if EARLY[j]:
            lb[j, at_line(x)] = lout[:, own]
        else:
            vb[j, at_line(x, WIN)] = lsv[:, own]
            qb[j, at_line(x)] = lsq[:, own]
    local(lout, lin_out, load.at[7])

    keep_first = jnp.logical_not(tri) | (
        lax.broadcasted_iota(jnp.int32, (QT, QT), 0) == lax.broadcasted_iota(jnp.int32, (QT, QT), 1)
    )
    key_at = lax.broadcasted_iota(jnp.int32, (QT, QT), 1)
    floor = jnp.where(r == 0, WIN, 0)
    scale = DH**-0.5 * LOG2E

    def tile(j, i, halo):
        start = pl.multiple_of(i * QT, QT)
        q = qb[j, pl.ds(start, QT), :]
        scores = nt(q, kb[j, pl.ds(start, KT), :])
        parts = []
        for t in range(KT // QT):
            part = scores[:, t * QT : (t + 1) * QT]
            keep = None
            if t == 0:
                keep = keep_first
            if t == KT // QT - 1:
                keep = tri
            if halo and t < WIN // QT:
                inside_line = key_at + (start + t * QT) >= floor
                keep = inside_line if keep is None else keep & inside_line
            parts.append(part if keep is None else jnp.where(keep, part, -jnp.inf))
        top = parts[0]
        for part in parts[1:]:
            top = jnp.maximum(top, part)
        top = jnp.max(top, axis=1, keepdims=True)
        raised = [jnp.exp2((part - top) * scale) for part in parts]
        whole = raised[0]
        for part in raised[1:]:
            whole = whole + part
        whole = jnp.sum(whole, axis=1, keepdims=True)
        probability = jnp.concatenate([part.astype(BF16) for part in raised], axis=1)
        out = nn(probability, vb[j, pl.ds(start, KT), :])
        ob[j, pl.ds(start, QT), :] = (out / whole).astype(BF16)

    def send_out(j, b):
        at = cols(x * G + j)
        src = ob.at[j, pl.ds(b * TOK, TOK)]

        @pl.when(b != x)
        def _():
            pltpu.make_async_remote_copy(
                src_ref=src, dst_ref=win_out.at[:, at], send_sem=osend.at[0],
                recv_sem=osem.at[0], device_id=(r * NX + b, h), device_id_type=MESH,
            ).start()

        @pl.when(b == x)
        def _():
            local(src, win_out.at[:, at], load.at[8])

    if any(EARLY):
        drain(qb.at[pl.ds(0, 2 * sum(EARLY)), pl.ds(0, TOK)], load.at[4])
    for j in range(G):
        three = kb.at[j, pl.ds(0, (NX - 1) * TOK)]
        drain(three, avsem.at[j, 1])
        drain(three, aqsem.at[j, 1])
        if EARLY[j]:
            drain(three, losem.at[j, 1])
            wide = lb[j].astype(F32)
            vb[j, pl.ds(WIN, LINE)] = (vb[j, pl.ds(WIN, LINE)].astype(F32) + wide).astype(BF16)
            qb[j] = (qb[j].astype(F32) + wide).astype(BF16)
        remote(vb.at[j, pl.ds(LINE, WIN)], vb.at[j, pl.ds(0, WIN)], vhsem.at[j], rdev(1))

        def later(i, carry):
            tile(j, i, False)
            return carry

        def first(i, carry):
            tile(j, i, True)
            return carry

        lax.fori_loop(WIN // QT, LINE // QT, later, 0)
        for b in range(WIN // TOK, NX):
            send_out(j, b)
        halo = kb.at[j, pl.ds(0, WIN)]
        drain(halo, khsem.at[j, 1])
        drain(halo, vhsem.at[j, 1])
        lax.fori_loop(0, WIN // QT, first, 0)
        for b in range(WIN // TOK):
            send_out(j, b)

    drain(lout, load.at[7])
    drain(kb.at[pl.ds(0, G), pl.ds(0, TOK)], load.at[8])
    rest = ob.at[pl.ds(0, NX - 1)]
    drain(rest, osem.at[0])
    drain(rest, osend.at[0])
    drain(totx.at[pl.ds(0, NX - 1)], tsem.at[0])
    drain(rowtots.at[pl.ds(0, NR - 1)], rtsem.at[0])
    drain(sx.at[pl.ds(0, NX - 1)], ssem.at[0])
    drain(trows.at[pl.ds(0, NR - 1)], trsem.at[0])
    drain(prow.at[pl.ds(0, NR - 1)], psem.at[0])
    drain(px.at[pl.ds(0, NX - 1)], xsem.at[0])
    drain(sqr.at[pl.ds(0, NHEAD - 1)], qsem.at[0])
    for j in range(G):
        three = kb.at[j, pl.ds(0, (NX - 1) * TOK)]
        halo = kb.at[j, pl.ds(0, WIN)]
        drain(three, ksem.at[j, 0])
        drain(halo, khsem.at[j, 0])
        drain(halo, vhsem.at[j, 0])
        drain(three, aqsem.at[j, 0])
        drain(three, avsem.at[j, 0])
        if EARLY[j]:
            drain(three, losem.at[j, 0])


def body(lin_query, lin_key, lin_value, log_decay, soft_query, soft_key, soft_value):
    wide = (TOK, H * DH)
    vmem, dma = pltpu.VMEM, pltpu.SemaphoreType.DMA
    hbm = pl.BlockSpec(memory_space=pl.ANY)
    return pl.pallas_call(
        kernel,
        out_shape=[jax.ShapeDtypeStruct(wide, BF16)] * 2,
        in_specs=[hbm] * 3 + [pl.BlockSpec(memory_space=vmem)] + [hbm] * 3,
        out_specs=[hbm, hbm],
        scratch_shapes=[vmem(wide, BF16)] * 6
        + [
            vmem((H, TOK), F32),
            vmem((H, TOK, DH), F32),
            vmem((H, TOK, DH), F32),
            vmem((TOK, DH), F32),
            vmem((H, DH), F32),
            vmem((NX, H, DH), F32),
            vmem((H, DH), F32),
            vmem((NR, H, DH), F32),
            vmem((H, DH, DH), BF16),
            vmem((NX, G, DH, DH), BF16),
            vmem((NR, DH // 4, DH), BF16),
            vmem((NR, DH // 4, DH), BF16),
            vmem((NR, DH // 4, DH), BF16),
            vmem((NR, DH // 4, DH), BF16),
            vmem((NX, G, DH, DH), BF16),
            vmem((H, DH, DH), BF16),
            vmem((8, TOK), F32),
            vmem((NHEAD, 8, TOK), F32),
            vmem((G, SPAN, DH), BF16),
            vmem((G, SPAN, DH), BF16),
            vmem((G, LINE, DH), BF16),
            vmem((G, LINE, DH), BF16),
            vmem((G, LINE, DH), BF16),
            dma((9,)),
        ]
        + [dma((2,))] * 7
        + [dma((G, 2))] * 6
        + [dma((1,)), dma((1,))],
        compiler_params=pltpu.CompilerParams(
            collective_id=1, has_side_effects=True, vmem_limit_bytes=48 * 2**20
        ),
        cost_estimate=pl.CostEstimate(
            flops=6 * 10**9, bytes_accessed=13 * 2**20, transcendentals=10**7
        ),
    )(lin_query, lin_key, lin_value, log_decay, soft_query, soft_key, soft_value)


def solution(mesh):
    spec = P("ctx", "head")
    return jax.shard_map(
        body,
        mesh=mesh,
        in_specs=(spec, spec, spec, P("head", "ctx"), spec, spec, spec),
        out_specs=(spec, spec),
        check_vma=False,
    )
```

```python
import jax
import jax.numpy as jnp
from jax import lax
from jax.experimental import pallas as pl
from jax.experimental.pallas import tpu as pltpu
from jax.sharding import PartitionSpec as P

MESH = pl.DeviceIdType.MESH
F32, BF16 = jnp.float32, jnp.bfloat16
DH = 128
H = 16
TOK = 384
NX = 4
NR = 16
NHEAD = 4
G = H // NX
WIN = 768
LINE = NX * TOK
SPAN = WIN + LINE
QT = 128
KT = WIN + QT
EARLY = (True, True, False, False)
STATES, PAIR, CARRY, TILES = 4, 2, 4, 3
SPLIT = (6, 4, 4, 2)
AHEAD = 4
LOG2E = 1.4426950408889634


def nt(a, b, **kw):
    return lax.dot_general(a, b, (((1,), (1,)), ((), ())), preferred_element_type=F32, **kw)


def tn(a, b):
    return lax.dot_general(a, b, (((0,), (0,)), ((), ())), preferred_element_type=F32)


def nn(a, b):
    return jnp.dot(a, b, preferred_element_type=F32)


def kernel(
    lq, lk, lv, ld, sq, sk, sv, lin_out, win_out,
    vq, vk, vv, lsq, lsv, lout, cumrow, colb, inside, acc,
    tot, totx, rowtot, rowtots, st, sx, tsrc, trows, pout, prow, px, pre,
    sqs, sqr, kb, vb, qb, lb, ob,
    load, tsem, rtsem, ssem, trsem, psem, xsem, qsem,
    ksem, khsem, vhsem, aqsem, avsem, losem, osem, osend,
    line_in, all_in,
):
    c = lax.axis_index("ctx")
    h = lax.axis_index("head")
    r, x = lax.div(c, NX), lax.rem(c, NX)

    def line(k):
        return lax.rem(x + k, NX)

    def row(k):
        return lax.rem(r + k, NR)

    def xdev(k):
        return (r * NX + line(k), h)

    def rdev(k):
        return (row(k) * NX + x, h)

    def hdev(k):
        return (c, lax.rem(h + k, NHEAD))

    def remote(src, dst, sems, dev):
        pltpu.make_async_remote_copy(
            src_ref=src, dst_ref=dst, send_sem=sems.at[0], recv_sem=sems.at[1],
            device_id=dev, device_id_type=MESH,
        ).start()

    def local(src, dst, sem):
        pltpu.make_async_copy(src, dst, sem).start()

    def drain(ref, sem):
        pltpu.make_async_copy(ref, ref, sem).wait()

    def repeat(first, count, step, f):
        def some(i, carry):
            for n in range(step):
                f(first + i * step + n)
            return carry

        lax.fori_loop(0, count // step, some, 0)

    def cols(head):
        return pl.ds(pl.multiple_of(head * DH, DH), DH)

    def at_line(k, base=0):
        return pl.ds(pl.multiple_of(base + k * TOK, TOK), TOK)

    barrier = pltpu.get_barrier_semaphore()

    def signal(sem, dev):
        pl.semaphore_signal(sem, inc=1, device_id=dev, device_id_type=MESH)

    @pl.when(x != 0)
    def _():
        for k in range(1, NX):

            @pl.when(line(k) != 0)
            def _():
                signal(barrier, xdev(k))

    @pl.when(x == 0)
    def _():
        for k in range(1, NX):
            signal(barrier, xdev(k))

    local(lk, vk, load.at[0])
    local(lv, vv, load.at[1])
    local(lq, vq, load.at[2])
    for j in range(G):
        own = cols(x * G + j)
        local(sk.at[:, own], kb.at[j, at_line(x, WIN)], load.at[3])
        if EARLY[j]:
            local(sq.at[:, own], qb.at[j, at_line(x)], load.at[4])
            local(sv.at[:, own], vb.at[j, at_line(x, WIN)], load.at[4])
    if not all(EARLY):
        local(sq, lsq, load.at[5])
        local(sv, lsv, load.at[6])

    decay = ld[...]
    at_row = lax.broadcasted_iota(jnp.int32, (TOK, TOK), 0)
    at_col = lax.broadcasted_iota(jnp.int32, (TOK, TOK), 1)
    lower = jnp.where(at_row >= at_col, 1.0, 0.0).astype(F32)
    cumrow[...] = nt(decay, lower, precision=lax.Precision.HIGHEST)
    cum_col = nt(lower, decay, precision=lax.Precision.HIGHEST)
    for hh in range(H):
        colb[hh] = jnp.broadcast_to(cum_col[:, hh : hh + 1], (TOK, DH))
    tot[...] = jnp.broadcast_to(jnp.sum(decay, axis=1, keepdims=True), (H, DH))
    totx[x] = tot[...]

    @pl.when(x != 0)
    def _():
        pl.semaphore_wait(barrier, NX - 1)
        signal(line_in, (r * NX, h))

    @pl.when(x == 0)
    def _():
        pl.semaphore_wait(line_in, NX - 1)
        for k in range(1, NHEAD):
            signal(barrier, hdev(k))

        def greet(k, carry):
            signal(barrier, rdev(k))
            return carry

        lax.fori_loop(1, NR, greet, 0)

    for k in range(1, NX):
        remote(tot, totx.at[x], tsem, xdev(k))

    def send_keys(j):
        for k in range(1, NX):
            remote(
                sk.at[:, cols(line(k) * G + j)], kb.at[j, at_line(x, WIN)], ksem.at[j], xdev(k)
            )

    send_keys(0)

    drain(vk, load.at[0])
    drain(vv, load.at[1])

    def state(hh):
        k = vk[:, cols(hh)].astype(F32)
        fall = jnp.exp(tot[pl.ds(hh, 1), :] - colb[hh])
        st[hh] = tn((k * fall).astype(BF16), vv[:, cols(hh)]).astype(BF16)

    for k in (2, 1, 3, 0):
        first = line(k) * G
        repeat(first, G, STATES, state)
        if k:
            remote(st.at[pl.ds(first, G)], sx.at[x], ssem, xdev(k))
    sx[x] = st[pl.ds(x * G, G)]
    send_keys(1)
    send_keys(2)
    send_keys(3)

    drain(totx.at[pl.ds(0, NX - 1)], tsem.at[1])
    whole_line = totx[0] + totx[1] + totx[2] + totx[3]
    rowtot[...] = jnp.broadcast_to(whole_line[:, None, :], rowtot.shape)
    rowtots[r] = rowtot[x * G + lax.div(r, NR // G)]

    @pl.when(x == 0)
    def _():
        pl.semaphore_wait(barrier, (NR - 1) + (NHEAD - 1))
        for k in range(1, NX):
            signal(all_in, xdev(k))

    @pl.when(x != 0)
    def _():
        pl.semaphore_wait(all_in, 1)

    def send_rowtot(k, carry):
        remote(rowtot.at[x * G + lax.div(row(k), NR // G)], rowtots.at[r], rtsem, rdev(k))
        return carry

    lax.fori_loop(1, NR, send_rowtot, 0)

    drain(vq, load.at[2])
    tri = lax.broadcasted_iota(jnp.int32, (QT, QT), 0) >= lax.broadcasted_iota(
        jnp.int32, (QT, QT), 1
    )

    def intra(hh):
        q, k, v = vq[:, cols(hh)], vk[:, cols(hh)], vv[:, cols(hh)]
        crow = cumrow[pl.ds(hh, 1), :]
        for i in range(TOK // QT):
            n = (i + 1) * QT
            scores = nt(q[i * QT : n], k[:n])
            cc = colb[hh, i * QT : n, :]
            parts = []
            for s in range(i + 1):
                gap = cc - crow[:, s * QT : (s + 1) * QT]
                if s == i:
                    gap = jnp.where(tri, gap, -jnp.inf)
                parts.append((scores[:, s * QT : (s + 1) * QT] * jnp.exp(gap)).astype(BF16))
            weights = jnp.concatenate(parts, axis=1) if i else parts[0]
            inside[hh, i * QT : n, :] = nn(weights, v[:n])
        colb[hh] = jnp.exp(colb[hh])

    repeat(0, SPLIT[0], PAIR, intra)

    drain(sx.at[pl.ds(0, NX - 1)], ssem.at[1])

    def line_sum(g, carry):
        total = jnp.zeros((DH, DH), F32)
        for s in range(NX):
            total = jnp.exp(totx[s, pl.ds(x * G + g, 1), :]) * total + sx[s, g].astype(F32)
        tsrc[pl.ds(g * 4, 4)] = total.astype(BF16).reshape(4, DH // 4, DH)
        return carry

    lax.fori_loop(0, G, line_sum, 0)
    trows[r] = tsrc[r]

    def send_sum(k, carry):
        remote(tsrc.at[row(k)], trows.at[r], trsem, rdev(k))
        return carry

    lax.fori_loop(1, NR, send_sum, 0)
    repeat(SPLIT[0], SPLIT[1], PAIR, intra)

    drain(rowtots.at[pl.ds(0, NR - 1)], rtsem.at[1])
    drain(trows.at[pl.ds(0, NR - 1)], trsem.at[1])

    def scan_rows(k, before):
        pout[k] = before.astype(BF16)
        return jnp.exp(rowtots[k, 0:1, :]) * before + trows[k].astype(F32)

    lax.fori_loop(0, NR, scan_rows, jnp.zeros((DH // 4, DH), F32))
    prow[r] = pout[r]

    def send_before(k, carry):
        remote(pout.at[row(k)], prow.at[r], psem, rdev(k))
        return carry

    lax.fori_loop(1, NR, send_before, 0)
    repeat(SPLIT[0] + SPLIT[1], SPLIT[2], PAIR, intra)
    drain(prow.at[pl.ds(0, NR - 1)], psem.at[1])

    def line_scan(g, carry):
        before = prow[pl.ds(g * 4, 4)].reshape(DH, DH).astype(F32)
        for s in range(NX):
            px[s, g] = before.astype(BF16)
            before = jnp.exp(totx[s, pl.ds(x * G + g, 1), :]) * before + sx[s, g].astype(F32)
        return carry

    lax.fori_loop(0, G, line_scan, 0)
    for k in (2, 1, 3):
        remote(px.at[line(k)], pre.at[pl.ds(x * G, G)], xsem.at[k - 1], xdev(k))
    pre[pl.ds(x * G, G)] = px[x]

    for j in range(G):
        if EARLY[j]:
            for k in range(1, NX):
                other = cols(line(k) * G + j)
                remote(sv.at[:, other], vb.at[j, at_line(x, WIN)], avsem.at[j], xdev(k))
                remote(sq.at[:, other], qb.at[j, at_line(x)], aqsem.at[j], xdev(k))

    drain(kb.at[pl.ds(0, G), pl.ds(0, TOK)], load.at[3])
    for j in range(G):
        drain(kb.at[j, pl.ds(0, (NX - 1) * TOK)], ksem.at[j, 1])
        remote(kb.at[j, pl.ds(LINE, WIN)], kb.at[j, pl.ds(0, WIN)], khsem.at[j], rdev(1))

    repeat(SPLIT[0] + SPLIT[1] + SPLIT[2], SPLIT[3], PAIR, intra)
    acc[...] = jnp.zeros_like(acc)

    def carry_in(hh):
        both = inside[hh] + nn(vq[:, cols(hh)], pre[hh]) * colb[hh]
        inside[hh] = both
        acc[...] += both * both

    for k in (0, 1, 3, 2):
        if k:
            drain(pre.at[pl.ds(0, G)], xsem.at[k - 1, 1])
        repeat(lax.rem(x + NX - k, NX) * G, G, CARRY, carry_in)
    eye = at_row == at_col
    squares = jnp.sum(acc[...], axis=1, keepdims=True)
    as_row = jnp.sum(jnp.where(eye, squares, 0.0), axis=0, keepdims=True)
    sqs[...] = jnp.broadcast_to(as_row, sqs.shape)
    for k in range(1, NHEAD):
        remote(sqs, sqr.at[h], qsem, hdev(k))
    sqr[h] = sqs[...]
    if not all(EARLY):
        drain(lsq, load.at[5])
        drain(lsv, load.at[6])
    drain(sqr.at[pl.ds(0, NHEAD - 1)], qsem.at[1])
    feature_sum = sqr[0] + sqr[1] + sqr[2] + sqr[3]
    inverse = lax.rsqrt(feature_sum / (NHEAD * H * DH) + 1e-05)[0:1, :]
    as_col = jnp.sum(jnp.where(eye, inverse, 0.0), axis=1, keepdims=True)
    acc[...] = jnp.broadcast_to(as_col, acc.shape)

    for j in range(G):

        def normalize(k):
            at = cols(k * G + j)
            out = (inside[k * G + j] * acc[...]).astype(BF16)
            lout[:, at] = out
            if not EARLY[j]:
                wide = out.astype(F32)
                lsq[:, at] = (lsq[:, at].astype(F32) + wide).astype(BF16)
                lsv[:, at] = (lsv[:, at].astype(F32) + wide).astype(BF16)

        repeat(0, NX, 2, normalize)
        own = cols(x * G + j)
        if EARLY[j]:
            lb[j, at_line(x)] = lout[:, own]
        else:
            vb[j, at_line(x, WIN)] = lsv[:, own]
            qb[j, at_line(x)] = lsq[:, own]
    local(lout, lin_out, load.at[7])

    def send_sums(j):
        for k in range(1, NX):
            other = cols(line(k) * G + j)
            if EARLY[j]:
                remote(lout.at[:, other], lb.at[j, at_line(x)], losem.at[j], xdev(k))
            else:
                remote(lsv.at[:, other], vb.at[j, at_line(x, WIN)], avsem.at[j], xdev(k))
                remote(lsq.at[:, other], qb.at[j, at_line(x)], aqsem.at[j], xdev(k))

    keep_first = jnp.logical_not(tri) | (
        lax.broadcasted_iota(jnp.int32, (QT, QT), 0) == lax.broadcasted_iota(jnp.int32, (QT, QT), 1)
    )
    key_at = lax.broadcasted_iota(jnp.int32, (QT, QT), 1)
    floor = jnp.where(r == 0, WIN, 0)
    scale = DH**-0.5 * LOG2E

    def tile(j, i, halo):
        start = pl.multiple_of(i * QT, QT)
        q = qb[j, pl.ds(start, QT), :]
        scores = nt(q, kb[j, pl.ds(start, KT), :])
        parts = []
        for t in range(KT // QT):
            part = scores[:, t * QT : (t + 1) * QT]
            keep = None
            if t == 0:
                keep = keep_first
            if t == KT // QT - 1:
                keep = tri
            if halo and t < WIN // QT:
                inside_line = key_at + (start + t * QT) >= floor
                keep = inside_line if keep is None else keep & inside_line
            parts.append(part if keep is None else jnp.where(keep, part, -jnp.inf))
        top = parts[0]
        for part in parts[1:]:
            top = jnp.maximum(top, part)
        top = jnp.max(top, axis=1, keepdims=True)
        raised = [jnp.exp2((part - top) * scale) for part in parts]
        whole = raised[0]
        for part in raised[1:]:
            whole = whole + part
        whole = jnp.sum(whole, axis=1, keepdims=True)
        probability = jnp.concatenate([part.astype(BF16) for part in raised], axis=1)
        out = nn(probability, vb[j, pl.ds(start, KT), :])
        ob[j, pl.ds(start, QT), :] = (out / whole).astype(BF16)

    def send_out(j, b):
        at = cols(x * G + j)
        src = ob.at[j, pl.ds(b * TOK, TOK)]

        @pl.when(b != x)
        def _():
            pltpu.make_async_remote_copy(
                src_ref=src, dst_ref=win_out.at[:, at], send_sem=osend.at[0],
                recv_sem=osem.at[0], device_id=(r * NX + b, h), device_id_type=MESH,
            ).start()

        @pl.when(b == x)
        def _():
            local(src, win_out.at[:, at], load.at[8])

    for j in range(AHEAD):
        send_sums(j)
    if any(EARLY):
        drain(qb.at[pl.ds(0, 2 * sum(EARLY)), pl.ds(0, TOK)], load.at[4])
    def arrive(j):
        three = kb.at[j, pl.ds(0, (NX - 1) * TOK)]
        drain(three, avsem.at[j, 1])
        drain(three, aqsem.at[j, 1])
        if EARLY[j]:
            drain(three, losem.at[j, 1])
        if j + AHEAD < G:
            send_sums(j + AHEAD)
        if EARLY[j]:
            wide = lb[j].astype(F32)
            vb[j, pl.ds(WIN, LINE)] = (vb[j, pl.ds(WIN, LINE)].astype(F32) + wide).astype(BF16)
            qb[j] = (qb[j].astype(F32) + wide).astype(BF16)
        remote(vb.at[j, pl.ds(LINE, WIN)], vb.at[j, pl.ds(0, WIN)], vhsem.at[j], rdev(1))

    def later(j):
        repeat(WIN // QT, (LINE - WIN) // QT, TILES, lambda i: tile(j, i, False))
        for b in range(WIN // TOK, NX):
            send_out(j, b)

    def first(j):
        halo = kb.at[j, pl.ds(0, WIN)]
        drain(halo, khsem.at[j, 1])
        drain(halo, vhsem.at[j, 1])
        repeat(0, WIN // QT, TILES, lambda i: tile(j, i, True))
        for b in range(WIN // TOK):
            send_out(j, b)

    for j in range(G):
        arrive(j)
        later(j)
        if j:
            first(j - 1)
    first(G - 1)

    drain(lout, load.at[7])
    drain(kb.at[pl.ds(0, G), pl.ds(0, TOK)], load.at[8])
    rest = ob.at[pl.ds(0, NX - 1)]
    drain(rest, osem.at[0])
    drain(rest, osend.at[0])
    drain(totx.at[pl.ds(0, NX - 1)], tsem.at[0])
    drain(rowtots.at[pl.ds(0, NR - 1)], rtsem.at[0])
    drain(sx.at[pl.ds(0, NX - 1)], ssem.at[0])
    drain(trows.at[pl.ds(0, NR - 1)], trsem.at[0])
    drain(prow.at[pl.ds(0, NR - 1)], psem.at[0])
    for k in range(NX - 1):
        drain(px.at[0], xsem.at[k, 0])
    drain(sqr.at[pl.ds(0, NHEAD - 1)], qsem.at[0])
    for j in range(G):
        three = kb.at[j, pl.ds(0, (NX - 1) * TOK)]
        halo = kb.at[j, pl.ds(0, WIN)]
        drain(three, ksem.at[j, 0])
        drain(halo, khsem.at[j, 0])
        drain(halo, vhsem.at[j, 0])
        drain(three, aqsem.at[j, 0])
        drain(three, avsem.at[j, 0])
        if EARLY[j]:
            drain(three, losem.at[j, 0])


def body(lin_query, lin_key, lin_value, log_decay, soft_query, soft_key, soft_value):
    wide = (TOK, H * DH)
    vmem, dma = pltpu.VMEM, pltpu.SemaphoreType.DMA
    hbm = pl.BlockSpec(memory_space=pl.ANY)
    return pl.pallas_call(
        kernel,
        out_shape=[jax.ShapeDtypeStruct(wide, BF16)] * 2,
        in_specs=[hbm] * 3 + [pl.BlockSpec(memory_space=vmem)] + [hbm] * 3,
        out_specs=[hbm, hbm],
        scratch_shapes=[vmem(wide, BF16)] * 6
        + [
            vmem((H, TOK), F32),
            vmem((H, TOK, DH), F32),
            vmem((H, TOK, DH), F32),
            vmem((TOK, DH), F32),
            vmem((H, DH), F32),
            vmem((NX, H, DH), F32),
            vmem((H, 8, DH), F32),
            vmem((NR, 8, DH), F32),
            vmem((H, DH, DH), BF16),
            vmem((NX, G, DH, DH), BF16),
            vmem((NR, DH // 4, DH), BF16),
            vmem((NR, DH // 4, DH), BF16),
            vmem((NR, DH // 4, DH), BF16),
            vmem((NR, DH // 4, DH), BF16),
            vmem((NX, G, DH, DH), BF16),
            vmem((H, DH, DH), BF16),
            vmem((8, TOK), F32),
            vmem((NHEAD, 8, TOK), F32),
            vmem((G, SPAN, DH), BF16),
            vmem((G, SPAN, DH), BF16),
            vmem((G, LINE, DH), BF16),
            vmem((G, LINE, DH), BF16),
            vmem((G, LINE, DH), BF16),
            dma((9,)),
        ]
        + [dma((2,))] * 5
        + [dma((NX - 1, 2)), dma((2,))]
        + [dma((G, 2))] * 6
        + [dma((1,)), dma((1,))]
        + [pltpu.SemaphoreType.REGULAR] * 2,
        compiler_params=pltpu.CompilerParams(
            collective_id=1, has_side_effects=True, vmem_limit_bytes=60 * 2**20
        ),
        cost_estimate=pl.CostEstimate(
            flops=6 * 10**9, bytes_accessed=13 * 2**20, transcendentals=10**7
        ),
    )(lin_query, lin_key, lin_value, log_decay, soft_query, soft_key, soft_value)


def solution(mesh):
    spec = P("ctx", "head")
    return jax.shard_map(
        body,
        mesh=mesh,
        in_specs=(spec, spec, spec, P("head", "ctx"), spec, spec, spec),
        out_specs=(spec, spec),
        check_vma=False,
    )
```

```python
import jax
import jax.numpy as jnp
from jax import lax
from jax.experimental import pallas as pl
from jax.experimental.pallas import tpu as pltpu
from jax.sharding import PartitionSpec as P

MESH = pl.DeviceIdType.MESH
F32, BF16 = jnp.float32, jnp.bfloat16
DH = 128
H = 16
TOK = 384
NX = 4
NR = 16
NHEAD = 4
G = H // NX
WIN = 768
LINE = NX * TOK
SPAN = WIN + LINE
QT = 128
KT = WIN + QT
EARLY = (True, True, False, False)
STATES, PAIR, CARRY, TILES = 4, 2, 4, 3
SPLIT = (6, 4, 4, 2)
LOG2E = 1.4426950408889634


def nt(a, b, **kw):
    return lax.dot_general(a, b, (((1,), (1,)), ((), ())), preferred_element_type=F32, **kw)


def tn(a, b):
    return lax.dot_general(a, b, (((0,), (0,)), ((), ())), preferred_element_type=F32)


def nn(a, b):
    return jnp.dot(a, b, preferred_element_type=F32)


def kernel(
    lq, lk, lv, ld, sq, sk, sv, lin_out, win_out,
    vq, vk, vv, lsq, lsv, lout, cumrow, colb, inside, acc,
    tot, totx, rowtot, rowtots, st, sx, tsrc, trows, pout, prow, px, pre,
    sqs, sqr, kb, vb, qb, lb, ob,
    load, tsem, rtsem, ssem, trsem, psem, xsem, qsem,
    ksem, khsem, vhsem, aqsem, avsem, losem, osem, osend,
    line_in, all_in,
):
    c = lax.axis_index("ctx")
    h = lax.axis_index("head")
    r, x = lax.div(c, NX), lax.rem(c, NX)

    def line(k):
        return lax.rem(x + k, NX)

    def row(k):
        return lax.rem(r + k, NR)

    def xdev(k):
        return (r * NX + line(k), h)

    def rdev(k):
        return (row(k) * NX + x, h)

    def hdev(k):
        return (c, lax.rem(h + k, NHEAD))

    def remote(src, dst, sems, dev):
        pltpu.make_async_remote_copy(
            src_ref=src, dst_ref=dst, send_sem=sems.at[0], recv_sem=sems.at[1],
            device_id=dev, device_id_type=MESH,
        ).start()

    def local(src, dst, sem):
        pltpu.make_async_copy(src, dst, sem).start()

    def drain(ref, sem):
        pltpu.make_async_copy(ref, ref, sem).wait()

    def repeat(first, count, step, f):
        def some(i, carry):
            for n in range(step):
                f(first + i * step + n)
            return carry

        lax.fori_loop(0, count // step, some, 0)

    def cols(head):
        return pl.ds(pl.multiple_of(head * DH, DH), DH)

    def at_line(k, base=0):
        return pl.ds(pl.multiple_of(base + k * TOK, TOK), TOK)

    barrier = pltpu.get_barrier_semaphore()

    def signal(sem, dev):
        pl.semaphore_signal(sem, inc=1, device_id=dev, device_id_type=MESH)

    @pl.when(x != 0)
    def _():
        for k in range(1, NX):

            @pl.when(line(k) != 0)
            def _():
                signal(barrier, xdev(k))

    @pl.when(x == 0)
    def _():
        for k in range(1, NX):
            signal(barrier, xdev(k))

    local(lk, vk, load.at[0])
    local(lv, vv, load.at[1])
    local(lq, vq, load.at[2])
    @pl.when(x != 0)
    def _():
        pl.semaphore_wait(barrier, NX - 1)
        signal(line_in, (r * NX, h))

    @pl.when(x == 0)
    def _():
        pl.semaphore_wait(line_in, NX - 1)
        for k in range(1, NHEAD):
            signal(barrier, hdev(k))

        def greet(k, carry):
            signal(barrier, rdev(k))
            return carry

        lax.fori_loop(1, NR, greet, 0)

    def send_keys(j):
        for k in range(1, NX):
            remote(
                sk.at[:, cols(line(k) * G + j)], kb.at[j, at_line(x, WIN)], ksem.at[j], xdev(k)
            )

    send_keys(0)

    for j in range(G):
        own = cols(x * G + j)
        local(sk.at[:, own], kb.at[j, at_line(x, WIN)], load.at[3])
        if EARLY[j]:
            local(sq.at[:, own], qb.at[j, at_line(x)], load.at[4])
            local(sv.at[:, own], vb.at[j, at_line(x, WIN)], load.at[4])
    if not all(EARLY):
        local(sq, lsq, load.at[5])
        local(sv, lsv, load.at[6])

    decay = ld[...]
    at_row = lax.broadcasted_iota(jnp.int32, (TOK, TOK), 0)
    at_col = lax.broadcasted_iota(jnp.int32, (TOK, TOK), 1)
    lower = jnp.where(at_row >= at_col, 1.0, 0.0).astype(F32)
    cumrow[...] = nt(decay, lower, precision=lax.Precision.HIGHEST)
    cum_col = nt(lower, decay, precision=lax.Precision.HIGHEST)
    for hh in range(H):
        colb[hh] = jnp.broadcast_to(cum_col[:, hh : hh + 1], (TOK, DH))
    tot[...] = jnp.broadcast_to(jnp.sum(decay, axis=1, keepdims=True), (H, DH))
    totx[x] = tot[...]

    for k in range(1, NX):
        remote(tot, totx.at[x], tsem, xdev(k))

    drain(vk, load.at[0])
    drain(vv, load.at[1])

    def state(hh):
        k = vk[:, cols(hh)].astype(F32)
        fall = jnp.exp(tot[pl.ds(hh, 1), :] - colb[hh])
        st[hh] = tn((k * fall).astype(BF16), vv[:, cols(hh)]).astype(BF16)

    for k in (2, 1, 3, 0):
        first = line(k) * G
        repeat(first, G, STATES, state)
        if k:
            remote(st.at[pl.ds(first, G)], sx.at[x], ssem, xdev(k))
    sx[x] = st[pl.ds(x * G, G)]
    send_keys(1)
    send_keys(2)
    send_keys(3)

    drain(totx.at[pl.ds(0, NX - 1)], tsem.at[1])
    whole_line = totx[0] + totx[1] + totx[2] + totx[3]
    rowtot[...] = jnp.broadcast_to(whole_line[:, None, :], rowtot.shape)
    rowtots[r] = rowtot[x * G + lax.div(r, NR // G)]

    @pl.when(x == 0)
    def _():
        pl.semaphore_wait(barrier, (NR - 1) + (NHEAD - 1))
        for k in range(1, NX):
            signal(all_in, xdev(k))

    @pl.when(x != 0)
    def _():
        pl.semaphore_wait(all_in, 1)

    def send_rowtot(k, carry):
        remote(rowtot.at[x * G + lax.div(row(k), NR // G)], rowtots.at[r], rtsem, rdev(k))
        return carry

    lax.fori_loop(1, NR, send_rowtot, 0)

    drain(vq, load.at[2])
    tri = lax.broadcasted_iota(jnp.int32, (QT, QT), 0) >= lax.broadcasted_iota(
        jnp.int32, (QT, QT), 1
    )

    def intra(hh):
        q, k, v = vq[:, cols(hh)], vk[:, cols(hh)], vv[:, cols(hh)]
        crow = cumrow[pl.ds(hh, 1), :]
        for i in range(TOK // QT):
            n = (i + 1) * QT
            scores = nt(q[i * QT : n], k[:n])
            cc = colb[hh, i * QT : n, :]
            parts = []
            for s in range(i + 1):
                gap = cc - crow[:, s * QT : (s + 1) * QT]
                if s == i:
                    gap = jnp.where(tri, gap, -jnp.inf)
                parts.append((scores[:, s * QT : (s + 1) * QT] * jnp.exp(gap)).astype(BF16))
            weights = jnp.concatenate(parts, axis=1) if i else parts[0]
            inside[hh, i * QT : n, :] = nn(weights, v[:n])
        colb[hh] = jnp.exp(colb[hh])

    repeat(0, SPLIT[0], PAIR, intra)

    drain(sx.at[pl.ds(0, NX - 1)], ssem.at[1])

    def line_sum(g, carry):
        total = jnp.zeros((DH, DH), F32)
        for s in range(NX):
            total = jnp.exp(totx[s, pl.ds(x * G + g, 1), :]) * total + sx[s, g].astype(F32)
        tsrc[pl.ds(g * 4, 4)] = total.astype(BF16).reshape(4, DH // 4, DH)
        return carry

    lax.fori_loop(0, G, line_sum, 0)
    trows[r] = tsrc[r]

    def send_sum(k, carry):
        remote(tsrc.at[row(k)], trows.at[r], trsem, rdev(k))
        return carry

    lax.fori_loop(1, NR, send_sum, 0)
    repeat(SPLIT[0], SPLIT[1], PAIR, intra)

    drain(rowtots.at[pl.ds(0, NR - 1)], rtsem.at[1])
    drain(trows.at[pl.ds(0, NR - 1)], trsem.at[1])

    def scan_rows(k, before):
        pout[k] = before.astype(BF16)
        return jnp.exp(rowtots[k, 0:1, :]) * before + trows[k].astype(F32)

    lax.fori_loop(0, NR, scan_rows, jnp.zeros((DH // 4, DH), F32))
    prow[r] = pout[r]

    def send_before(k, carry):
        remote(pout.at[row(k)], prow.at[r], psem, rdev(k))
        return carry

    lax.fori_loop(1, NR, send_before, 0)
    repeat(SPLIT[0] + SPLIT[1], SPLIT[2], PAIR, intra)
    drain(prow.at[pl.ds(0, NR - 1)], psem.at[1])

    def line_scan(g, carry):
        before = prow[pl.ds(g * 4, 4)].reshape(DH, DH).astype(F32)
        for s in range(NX):
            px[s, g] = before.astype(BF16)
            before = jnp.exp(totx[s, pl.ds(x * G + g, 1), :]) * before + sx[s, g].astype(F32)
        return carry

    lax.fori_loop(0, G, line_scan, 0)
    for k in (2, 1, 3):
        remote(px.at[line(k)], pre.at[pl.ds(x * G, G)], xsem.at[k - 1], xdev(k))
    pre[pl.ds(x * G, G)] = px[x]

    for j in range(G):
        if EARLY[j]:
            for k in range(1, NX):
                other = cols(line(k) * G + j)
                remote(sv.at[:, other], vb.at[j, at_line(x, WIN)], avsem.at[j], xdev(k))
                remote(sq.at[:, other], qb.at[j, at_line(x)], aqsem.at[j], xdev(k))

    def to_next(part, sems):
        @pl.when(r < NR - 1)
        def _():
            remote(part.at[pl.ds(LINE, WIN)], part.at[pl.ds(0, WIN)], sems, rdev(1))

    @pl.when(r == 0)
    def _():
        kb[:, 0:WIN, :] = jnp.zeros((G, WIN, DH), BF16)
        vb[:, 0:WIN, :] = jnp.zeros((G, WIN, DH), BF16)

    drain(kb.at[pl.ds(0, G), pl.ds(0, TOK)], load.at[3])
    for j in range(G):
        drain(kb.at[j, pl.ds(0, (NX - 1) * TOK)], ksem.at[j, 1])
        to_next(kb.at[j], khsem.at[j])

    repeat(SPLIT[0] + SPLIT[1] + SPLIT[2], SPLIT[3], PAIR, intra)
    acc[...] = jnp.zeros_like(acc)

    def carry_in(hh):
        both = inside[hh] + nn(vq[:, cols(hh)], pre[hh]) * colb[hh]
        inside[hh] = both
        acc[...] += both * both

    for k in (0, 1, 3, 2):
        if k:
            drain(pre.at[pl.ds(0, G)], xsem.at[k - 1, 1])
        repeat(lax.rem(x + NX - k, NX) * G, G, CARRY, carry_in)
    eye = at_row == at_col
    squares = jnp.sum(acc[...], axis=1, keepdims=True)
    as_row = jnp.sum(jnp.where(eye, squares, 0.0), axis=0, keepdims=True)
    sqs[...] = jnp.broadcast_to(as_row, sqs.shape)
    for k in range(1, NHEAD):
        remote(sqs, sqr.at[h], qsem, hdev(k))
    sqr[h] = sqs[...]
    if not all(EARLY):
        drain(lsq, load.at[5])
        drain(lsv, load.at[6])
    drain(sqr.at[pl.ds(0, NHEAD - 1)], qsem.at[1])
    feature_sum = sqr[0] + sqr[1] + sqr[2] + sqr[3]
    inverse = lax.rsqrt(feature_sum / (NHEAD * H * DH) + 1e-05)[0:1, :]
    as_col = jnp.sum(jnp.where(eye, inverse, 0.0), axis=1, keepdims=True)
    acc[...] = jnp.broadcast_to(as_col, acc.shape)

    def send_sums(j):
        for k in range(1, NX):
            other = cols(line(k) * G + j)
            if EARLY[j]:
                remote(lout.at[:, other], lb.at[j, at_line(x)], losem.at[j], xdev(k))
            else:
                remote(lsv.at[:, other], vb.at[j, at_line(x, WIN)], avsem.at[j], xdev(k))
                remote(lsq.at[:, other], qb.at[j, at_line(x)], aqsem.at[j], xdev(k))

    for j in range(G):

        def normalize(k):
            at = cols(k * G + j)
            out = (inside[k * G + j] * acc[...]).astype(BF16)
            lout[:, at] = out
            if not EARLY[j]:
                wide = out.astype(F32)
                lsq[:, at] = (lsq[:, at].astype(F32) + wide).astype(BF16)
                lsv[:, at] = (lsv[:, at].astype(F32) + wide).astype(BF16)

        repeat(0, NX, 2, normalize)
        send_sums(j)
        own = cols(x * G + j)
        if EARLY[j]:
            lb[j, at_line(x)] = lout[:, own]
        else:
            vb[j, at_line(x, WIN)] = lsv[:, own]
            qb[j, at_line(x)] = lsq[:, own]
    local(lout, lin_out, load.at[7])

    keep_first = jnp.logical_not(tri) | (
        lax.broadcasted_iota(jnp.int32, (QT, QT), 0) == lax.broadcasted_iota(jnp.int32, (QT, QT), 1)
    )
    key_at = lax.broadcasted_iota(jnp.int32, (QT, QT), 1)
    floor = jnp.where(r == 0, WIN, 0)
    scale = DH**-0.5 * LOG2E

    def tile(j, i, halo):
        start = pl.multiple_of(i * QT, QT)
        q = qb[j, pl.ds(start, QT), :]
        scores = nt(q, kb[j, pl.ds(start, KT), :])
        parts = []
        for t in range(KT // QT):
            part = scores[:, t * QT : (t + 1) * QT]
            keep = None
            if t == 0:
                keep = keep_first
            if t == KT // QT - 1:
                keep = tri
            if halo and t < WIN // QT:
                inside_line = key_at + (start + t * QT) >= floor
                keep = inside_line if keep is None else keep & inside_line
            parts.append(part if keep is None else jnp.where(keep, part, -jnp.inf))
        top = parts[0]
        for part in parts[1:]:
            top = jnp.maximum(top, part)
        top = jnp.max(top, axis=1, keepdims=True)
        raised = [jnp.exp2((part - top) * scale) for part in parts]
        whole = raised[0]
        for part in raised[1:]:
            whole = whole + part
        whole = jnp.sum(whole, axis=1, keepdims=True)
        probability = jnp.concatenate([part.astype(BF16) for part in raised], axis=1)
        out = nn(probability, vb[j, pl.ds(start, KT), :])
        ob[j, pl.ds(start, QT), :] = (out / whole).astype(BF16)

    def send_out(j, b):
        at = cols(x * G + j)
        src = ob.at[j, pl.ds(b * TOK, TOK)]

        @pl.when(b != x)
        def _():
            pltpu.make_async_remote_copy(
                src_ref=src, dst_ref=win_out.at[:, at], send_sem=osend.at[0],
                recv_sem=osem.at[0], device_id=(r * NX + b, h), device_id_type=MESH,
            ).start()

        @pl.when(b == x)
        def _():
            local(src, win_out.at[:, at], load.at[8])

    if any(EARLY):
        drain(qb.at[pl.ds(0, 2 * sum(EARLY)), pl.ds(0, TOK)], load.at[4])
    def arrive(j):
        three = kb.at[j, pl.ds(0, (NX - 1) * TOK)]
        drain(three, avsem.at[j, 1])
        drain(three, aqsem.at[j, 1])
        if EARLY[j]:
            drain(three, losem.at[j, 1])
        if EARLY[j]:
            wide = lb[j].astype(F32)
            vb[j, pl.ds(WIN, LINE)] = (vb[j, pl.ds(WIN, LINE)].astype(F32) + wide).astype(BF16)
            qb[j] = (qb[j].astype(F32) + wide).astype(BF16)
        to_next(vb.at[j], vhsem.at[j])

    def later(j):
        repeat(WIN // QT, (LINE - WIN) // QT, TILES, lambda i: tile(j, i, False))
        for b in range(WIN // TOK, NX):
            send_out(j, b)

    def first(j):
        @pl.when(r > 0)
        def _():
            halo = kb.at[j, pl.ds(0, WIN)]
            drain(halo, khsem.at[j, 1])
            drain(halo, vhsem.at[j, 1])

        repeat(0, WIN // QT, TILES, lambda i: tile(j, i, True))
        for b in range(WIN // TOK):
            send_out(j, b)

    for j in range(G):
        arrive(j)
        later(j)
        if j:
            first(j - 1)
    first(G - 1)

    drain(lout, load.at[7])
    drain(kb.at[pl.ds(0, G), pl.ds(0, TOK)], load.at[8])
    rest = ob.at[pl.ds(0, NX - 1)]
    drain(rest, osem.at[0])
    drain(rest, osend.at[0])
    drain(totx.at[pl.ds(0, NX - 1)], tsem.at[0])
    drain(rowtots.at[pl.ds(0, NR - 1)], rtsem.at[0])
    drain(sx.at[pl.ds(0, NX - 1)], ssem.at[0])
    drain(trows.at[pl.ds(0, NR - 1)], trsem.at[0])
    drain(prow.at[pl.ds(0, NR - 1)], psem.at[0])
    for k in range(NX - 1):
        drain(px.at[0], xsem.at[k, 0])
    drain(sqr.at[pl.ds(0, NHEAD - 1)], qsem.at[0])
    for j in range(G):
        three = kb.at[j, pl.ds(0, (NX - 1) * TOK)]
        drain(three, ksem.at[j, 0])

        @pl.when(r < NR - 1)
        def _():
            halo = kb.at[j, pl.ds(0, WIN)]
            drain(halo, khsem.at[j, 0])
            drain(halo, vhsem.at[j, 0])

        drain(three, aqsem.at[j, 0])
        drain(three, avsem.at[j, 0])
        if EARLY[j]:
            drain(three, losem.at[j, 0])


def body(lin_query, lin_key, lin_value, log_decay, soft_query, soft_key, soft_value):
    wide = (TOK, H * DH)
    vmem, dma = pltpu.VMEM, pltpu.SemaphoreType.DMA
    hbm = pl.BlockSpec(memory_space=pltpu.HBM)
    return pl.pallas_call(
        kernel,
        out_shape=[jax.ShapeDtypeStruct(wide, BF16)] * 2,
        in_specs=[hbm] * 3 + [pl.BlockSpec(memory_space=vmem)] + [hbm] * 3,
        out_specs=[hbm, hbm],
        scratch_shapes=[vmem(wide, BF16)] * 6
        + [
            vmem((H, TOK), F32),
            vmem((H, TOK, DH), F32),
            vmem((H, TOK, DH), F32),
            vmem((TOK, DH), F32),
            vmem((H, DH), F32),
            vmem((NX, H, DH), F32),
            vmem((H, 8, DH), F32),
            vmem((NR, 8, DH), F32),
            vmem((H, DH, DH), BF16),
            vmem((NX, G, DH, DH), BF16),
            vmem((NR, DH // 4, DH), BF16),
            vmem((NR, DH // 4, DH), BF16),
            vmem((NR, DH // 4, DH), BF16),
            vmem((NR, DH // 4, DH), BF16),
            vmem((NX, G, DH, DH), BF16),
            vmem((H, DH, DH), BF16),
            vmem((8, TOK), F32),
            vmem((NHEAD, 8, TOK), F32),
            vmem((G, SPAN, DH), BF16),
            vmem((G, SPAN, DH), BF16),
            vmem((G, LINE, DH), BF16),
            vmem((G, LINE, DH), BF16),
            vmem((G, LINE, DH), BF16),
            dma((9,)),
        ]
        + [dma((2,))] * 5
        + [dma((NX - 1, 2)), dma((2,))]
        + [dma((G, 2))] * 6
        + [dma((1,)), dma((1,))]
        + [pltpu.SemaphoreType.REGULAR] * 2,
        compiler_params=pltpu.CompilerParams(
            collective_id=1, has_side_effects=True, vmem_limit_bytes=60 * 2**20
        ),
        cost_estimate=pl.CostEstimate(
            flops=6 * 10**9, bytes_accessed=13 * 2**20, transcendentals=10**7
        ),
    )(lin_query, lin_key, lin_value, log_decay, soft_query, soft_key, soft_value)


def solution(mesh):
    spec = P("ctx", "head")
    return jax.shard_map(
        body,
        mesh=mesh,
        in_specs=(spec, spec, spec, P("head", "ctx"), spec, spec, spec),
        out_specs=(spec, spec),
        check_vma=False,
    )
```

```python
import jax
import jax.numpy as jnp
from jax import lax
from jax.experimental import pallas as pl
from jax.experimental.pallas import tpu as pltpu
from jax.sharding import PartitionSpec as P

MESH = pl.DeviceIdType.MESH
F32, BF16 = jnp.float32, jnp.bfloat16
DH = 128
H = 16
TOK = 384
NX = 4
NR = 16
NHEAD = 4
G = H // NX
WIN = 768
LINE = NX * TOK
SPAN = WIN + LINE
QT = 128
KT = WIN + QT
EARLY = (True, True, False, False)
STATES, PAIR, CARRY, TILES = 4, 2, 4, 3
SPLIT = (6, 4, 4, 2)
LOG2E = 1.4426950408889634


def nt(a, b, **kw):
    return lax.dot_general(a, b, (((1,), (1,)), ((), ())), preferred_element_type=F32, **kw)


def tn(a, b):
    return lax.dot_general(a, b, (((0,), (0,)), ((), ())), preferred_element_type=F32)


def nn(a, b):
    return jnp.dot(a, b, preferred_element_type=F32)


def kernel(
    lq, lk, lv, ld, sq, sk, sv, lin_out, win_out,
    vq, vk, vv, lsq, lsv, lout, cumrow, colb, inside, acc,
    tot, totx, rowtot, rowtots, st, sx, tsrc, trows, pout, prow, px, pre,
    sqs, sqr, kb, vb, qb, lb, ob,
    load, tsem, rtsem, ssem, trsem, psem, xsem, qsem,
    ksem, khsem, vhsem, aqsem, avsem, losem, osem, osend,
    line_in, all_in,
):
    c = lax.axis_index("ctx")
    h = lax.axis_index("head")
    r, x = lax.div(c, NX), lax.rem(c, NX)

    def line(k):
        return lax.rem(x + k, NX)

    def row(k):
        return lax.rem(r + k, NR)

    def xdev(k):
        return (r * NX + line(k), h)

    def rdev(k):
        return (row(k) * NX + x, h)

    def hdev(k):
        return (c, lax.rem(h + k, NHEAD))

    def remote(src, dst, sems, dev):
        pltpu.make_async_remote_copy(
            src_ref=src, dst_ref=dst, send_sem=sems.at[0], recv_sem=sems.at[1],
            device_id=dev, device_id_type=MESH,
        ).start()

    def local(src, dst, sem):
        pltpu.make_async_copy(src, dst, sem).start()

    def drain(ref, sem):
        pltpu.make_async_copy(ref, ref, sem).wait()

    def repeat(first, count, step, f):
        def some(i, carry):
            for n in range(step):
                f(first + i * step + n)
            return carry

        lax.fori_loop(0, count // step, some, 0)

    def cols(head):
        return pl.ds(pl.multiple_of(head * DH, DH), DH)

    def at_line(k, base=0):
        return pl.ds(pl.multiple_of(base + k * TOK, TOK), TOK)

    barrier = pltpu.get_barrier_semaphore()

    def signal(sem, dev):
        pl.semaphore_signal(sem, inc=1, device_id=dev, device_id_type=MESH)

    @pl.when(x != 0)
    def _():
        for k in range(1, NX):

            @pl.when(line(k) != 0)
            def _():
                signal(barrier, xdev(k))

    @pl.when(x == 0)
    def _():
        for k in range(1, NX):
            signal(barrier, xdev(k))

    local(lk, vk, load.at[0])
    local(lv, vv, load.at[1])
    local(lq, vq, load.at[2])
    @pl.when(x != 0)
    def _():
        pl.semaphore_wait(barrier, NX - 1)
        signal(line_in, (r * NX, h))

    @pl.when(x == 0)
    def _():
        pl.semaphore_wait(line_in, NX - 1)
        for k in range(1, NHEAD):
            signal(barrier, hdev(k))

        def greet(k, carry):
            signal(barrier, rdev(k))
            return carry

        lax.fori_loop(1, NR, greet, 0)

    def send_keys(j):
        for k in range(1, NX):
            remote(
                sk.at[:, cols(line(k) * G + j)], kb.at[j, at_line(x, WIN)], ksem.at[j], xdev(k)
            )

    send_keys(0)

    for j in range(G):
        own = cols(x * G + j)
        local(sk.at[:, own], kb.at[j, at_line(x, WIN)], load.at[3])
        if EARLY[j]:
            local(sq.at[:, own], qb.at[j, at_line(x)], load.at[4])
            local(sv.at[:, own], vb.at[j, at_line(x, WIN)], load.at[4])
    if not all(EARLY):
        local(sq, lsq, load.at[5])
        local(sv, lsv, load.at[6])

    decay = ld[...]
    at_row = lax.broadcasted_iota(jnp.int32, (TOK, TOK), 0)
    at_col = lax.broadcasted_iota(jnp.int32, (TOK, TOK), 1)
    lower = jnp.where(at_row >= at_col, 1.0, 0.0).astype(F32)
    cumrow[...] = nt(decay, lower, precision=lax.Precision.HIGHEST)
    cum_col = nt(lower, decay, precision=lax.Precision.HIGHEST)
    for hh in range(H):
        colb[hh] = jnp.broadcast_to(cum_col[:, hh : hh + 1], (TOK, DH))
    tot[...] = jnp.broadcast_to(jnp.sum(decay, axis=1, keepdims=True), (H, DH))
    totx[x] = tot[...]

    for k in range(1, NX):
        remote(tot, totx.at[x], tsem, xdev(k))

    drain(vk, load.at[0])
    drain(vv, load.at[1])

    def state(hh):
        k = vk[:, cols(hh)].astype(F32)
        fall = jnp.exp(tot[pl.ds(hh, 1), :] - colb[hh])
        st[hh] = tn((k * fall).astype(BF16), vv[:, cols(hh)]).astype(BF16)

    for k in (2, 1, 3, 0):
        first = line(k) * G
        repeat(first, G, STATES, state)
        if k:
            remote(st.at[pl.ds(first, G)], sx.at[x], ssem, xdev(k))
    sx[x] = st[pl.ds(x * G, G)]
    send_keys(1)
    send_keys(2)
    send_keys(3)

    def send_inputs(j):
        for k in range(1, NX):
            other = cols(line(k) * G + j)
            remote(sv.at[:, other], vb.at[j, at_line(x, WIN)], avsem.at[j], xdev(k))
            remote(sq.at[:, other], qb.at[j, at_line(x)], aqsem.at[j], xdev(k))

    @pl.when(r < NR // 2)
    def _():
        send_inputs(0)


    drain(totx.at[pl.ds(0, NX - 1)], tsem.at[1])
    whole_line = totx[0] + totx[1] + totx[2] + totx[3]
    rowtot[...] = jnp.broadcast_to(whole_line[:, None, :], rowtot.shape)
    rowtots[r] = rowtot[x * G + lax.div(r, NR // G)]

    @pl.when(x == 0)
    def _():
        pl.semaphore_wait(barrier, (NR - 1) + (NHEAD - 1))
        for k in range(1, NX):
            signal(all_in, xdev(k))

    @pl.when(x != 0)
    def _():
        pl.semaphore_wait(all_in, 1)

    def send_rowtot(k, carry):
        remote(rowtot.at[x * G + lax.div(row(k), NR // G)], rowtots.at[r], rtsem, rdev(k))
        return carry

    lax.fori_loop(1, NR, send_rowtot, 0)

    drain(vq, load.at[2])
    tri = lax.broadcasted_iota(jnp.int32, (QT, QT), 0) >= lax.broadcasted_iota(
        jnp.int32, (QT, QT), 1
    )

    def intra(hh):
        q, k, v = vq[:, cols(hh)], vk[:, cols(hh)], vv[:, cols(hh)]
        crow = cumrow[pl.ds(hh, 1), :]
        for i in range(TOK // QT):
            n = (i + 1) * QT
            scores = nt(q[i * QT : n], k[:n])
            cc = colb[hh, i * QT : n, :]
            parts = []
            for s in range(i + 1):
                gap = cc - crow[:, s * QT : (s + 1) * QT]
                if s == i:
                    gap = jnp.where(tri, gap, -jnp.inf)
                parts.append((scores[:, s * QT : (s + 1) * QT] * jnp.exp(gap)).astype(BF16))
            weights = jnp.concatenate(parts, axis=1) if i else parts[0]
            inside[hh, i * QT : n, :] = nn(weights, v[:n])
        colb[hh] = jnp.exp(colb[hh])

    repeat(0, SPLIT[0], PAIR, intra)

    drain(sx.at[pl.ds(0, NX - 1)], ssem.at[1])

    def line_sum(g, carry):
        total = jnp.zeros((DH, DH), F32)
        for s in range(NX):
            total = jnp.exp(totx[s, pl.ds(x * G + g, 1), :]) * total + sx[s, g].astype(F32)
        tsrc[pl.ds(g * 4, 4)] = total.astype(BF16).reshape(4, DH // 4, DH)
        return carry

    lax.fori_loop(0, G, line_sum, 0)
    trows[r] = tsrc[r]

    def send_sum(k, carry):
        remote(tsrc.at[row(k)], trows.at[r], trsem, rdev(k))
        return carry

    lax.fori_loop(1, NR, send_sum, 0)
    repeat(SPLIT[0], SPLIT[1], PAIR, intra)

    drain(rowtots.at[pl.ds(0, NR - 1)], rtsem.at[1])
    drain(trows.at[pl.ds(0, NR - 1)], trsem.at[1])

    def scan_rows(k, before):
        pout[k] = before.astype(BF16)
        return jnp.exp(rowtots[k, 0:1, :]) * before + trows[k].astype(F32)

    lax.fori_loop(0, NR, scan_rows, jnp.zeros((DH // 4, DH), F32))
    prow[r] = pout[r]

    def send_before(k, carry):
        remote(pout.at[row(k)], prow.at[r], psem, rdev(k))
        return carry

    lax.fori_loop(1, NR, send_before, 0)
    repeat(SPLIT[0] + SPLIT[1], SPLIT[2], PAIR, intra)
    drain(prow.at[pl.ds(0, NR - 1)], psem.at[1])

    def line_scan(g, carry):
        before = prow[pl.ds(g * 4, 4)].reshape(DH, DH).astype(F32)
        for s in range(NX):
            px[s, g] = before.astype(BF16)
            before = jnp.exp(totx[s, pl.ds(x * G + g, 1), :]) * before + sx[s, g].astype(F32)
        return carry

    lax.fori_loop(0, G, line_scan, 0)
    for k in (2, 1, 3):
        remote(px.at[line(k)], pre.at[pl.ds(x * G, G)], xsem.at[k - 1], xdev(k))
    pre[pl.ds(x * G, G)] = px[x]

    for j in range(G):
        if EARLY[j] and j:
            send_inputs(j)

    @pl.when(r >= NR // 2)
    def _():
        send_inputs(0)

    def to_next(part, sems):
        @pl.when(r < NR - 1)
        def _():
            remote(part.at[pl.ds(LINE, WIN)], part.at[pl.ds(0, WIN)], sems, rdev(1))

    @pl.when(r == 0)
    def _():
        kb[:, 0:WIN, :] = jnp.zeros((G, WIN, DH), BF16)
        vb[:, 0:WIN, :] = jnp.zeros((G, WIN, DH), BF16)

    drain(kb.at[pl.ds(0, G), pl.ds(0, TOK)], load.at[3])
    for j in range(G):
        drain(kb.at[j, pl.ds(0, (NX - 1) * TOK)], ksem.at[j, 1])
        to_next(kb.at[j], khsem.at[j])

    repeat(SPLIT[0] + SPLIT[1] + SPLIT[2], SPLIT[3], PAIR, intra)
    acc[...] = jnp.zeros_like(acc)

    def carry_in(hh):
        both = inside[hh] + nn(vq[:, cols(hh)], pre[hh]) * colb[hh]
        inside[hh] = both
        acc[...] += both * both

    for k in (0, 1, 3, 2):
        if k:
            drain(pre.at[pl.ds(0, G)], xsem.at[k - 1, 1])
        repeat(lax.rem(x + NX - k, NX) * G, G, CARRY, carry_in)
    eye = at_row == at_col
    squares = jnp.sum(acc[...], axis=1, keepdims=True)
    as_row = jnp.sum(jnp.where(eye, squares, 0.0), axis=0, keepdims=True)
    sqs[...] = jnp.broadcast_to(as_row, sqs.shape)
    for k in range(1, NHEAD):
        remote(sqs, sqr.at[h], qsem, hdev(k))
    sqr[h] = sqs[...]
    if not all(EARLY):
        drain(lsq, load.at[5])
        drain(lsv, load.at[6])
    drain(sqr.at[pl.ds(0, NHEAD - 1)], qsem.at[1])
    feature_sum = sqr[0] + sqr[1] + sqr[2] + sqr[3]
    inverse = lax.rsqrt(feature_sum / (NHEAD * H * DH) + 1e-05)[0:1, :]
    as_col = jnp.sum(jnp.where(eye, inverse, 0.0), axis=1, keepdims=True)
    acc[...] = jnp.broadcast_to(as_col, acc.shape)

    def send_sums(j):
        for k in range(1, NX):
            other = cols(line(k) * G + j)
            if EARLY[j]:
                remote(lout.at[:, other], lb.at[j, at_line(x)], losem.at[j], xdev(k))
            else:
                remote(lsv.at[:, other], vb.at[j, at_line(x, WIN)], avsem.at[j], xdev(k))
                remote(lsq.at[:, other], qb.at[j, at_line(x)], aqsem.at[j], xdev(k))

    for j in range(G):

        def normalize(k):
            at = cols(k * G + j)
            out = (inside[k * G + j] * acc[...]).astype(BF16)
            lout[:, at] = out
            if not EARLY[j]:
                wide = out.astype(F32)
                lsq[:, at] = (lsq[:, at].astype(F32) + wide).astype(BF16)
                lsv[:, at] = (lsv[:, at].astype(F32) + wide).astype(BF16)

        repeat(0, NX, 2, normalize)
        send_sums(j)
        own = cols(x * G + j)
        if EARLY[j]:
            lb[j, at_line(x)] = lout[:, own]
        else:
            vb[j, at_line(x, WIN)] = lsv[:, own]
            qb[j, at_line(x)] = lsq[:, own]
    local(lout, lin_out, load.at[7])

    keep_first = jnp.logical_not(tri) | (
        lax.broadcasted_iota(jnp.int32, (QT, QT), 0) == lax.broadcasted_iota(jnp.int32, (QT, QT), 1)
    )
    key_at = lax.broadcasted_iota(jnp.int32, (QT, QT), 1)
    floor = jnp.where(r == 0, WIN, 0)
    scale = DH**-0.5 * LOG2E

    def tile(j, i, halo):
        start = pl.multiple_of(i * QT, QT)
        q = qb[j, pl.ds(start, QT), :]
        scores = nt(q, kb[j, pl.ds(start, KT), :])
        parts = []
        for t in range(KT // QT):
            part = scores[:, t * QT : (t + 1) * QT]
            keep = None
            if t == 0:
                keep = keep_first
            if t == KT // QT - 1:
                keep = tri
            if halo and t < WIN // QT:
                inside_line = key_at + (start + t * QT) >= floor
                keep = inside_line if keep is None else keep & inside_line
            parts.append(part if keep is None else jnp.where(keep, part, -jnp.inf))
        top = parts[0]
        for part in parts[1:]:
            top = jnp.maximum(top, part)
        top = jnp.max(top, axis=1, keepdims=True)
        raised = [jnp.exp2((part - top) * scale) for part in parts]
        whole = raised[0]
        for part in raised[1:]:
            whole = whole + part
        whole = jnp.sum(whole, axis=1, keepdims=True)
        probability = jnp.concatenate([part.astype(BF16) for part in raised], axis=1)
        out = nn(probability, vb[j, pl.ds(start, KT), :])
        ob[j, pl.ds(start, QT), :] = (out / whole).astype(BF16)

    def send_out(j, b):
        at = cols(x * G + j)
        src = ob.at[j, pl.ds(b * TOK, TOK)]

        @pl.when(b != x)
        def _():
            pltpu.make_async_remote_copy(
                src_ref=src, dst_ref=win_out.at[:, at], send_sem=osend.at[0],
                recv_sem=osem.at[0], device_id=(r * NX + b, h), device_id_type=MESH,
            ).start()

        @pl.when(b == x)
        def _():
            local(src, win_out.at[:, at], load.at[8])

    if any(EARLY):
        drain(qb.at[pl.ds(0, 2 * sum(EARLY)), pl.ds(0, TOK)], load.at[4])
    def arrive(j):
        three = kb.at[j, pl.ds(0, (NX - 1) * TOK)]
        drain(three, avsem.at[j, 1])
        drain(three, aqsem.at[j, 1])
        if EARLY[j]:
            drain(three, losem.at[j, 1])
        if EARLY[j]:
            wide = lb[j].astype(F32)
            vb[j, pl.ds(WIN, LINE)] = (vb[j, pl.ds(WIN, LINE)].astype(F32) + wide).astype(BF16)
            qb[j] = (qb[j].astype(F32) + wide).astype(BF16)
        to_next(vb.at[j], vhsem.at[j])

    def later(j):
        repeat(WIN // QT, (LINE - WIN) // QT, TILES, lambda i: tile(j, i, False))
        for b in range(WIN // TOK, NX):
            send_out(j, b)

    def first(j):
        @pl.when(r > 0)
        def _():
            halo = kb.at[j, pl.ds(0, WIN)]
            drain(halo, khsem.at[j, 1])
            drain(halo, vhsem.at[j, 1])

        repeat(0, WIN // QT, TILES, lambda i: tile(j, i, True))
        for b in range(WIN // TOK):
            send_out(j, b)

    for j in range(G):
        arrive(j)
        later(j)
        if j:
            first(j - 1)
    first(G - 1)

    drain(lout, load.at[7])
    drain(kb.at[pl.ds(0, G), pl.ds(0, TOK)], load.at[8])
    rest = ob.at[pl.ds(0, NX - 1)]
    drain(rest, osem.at[0])
    drain(rest, osend.at[0])
    drain(totx.at[pl.ds(0, NX - 1)], tsem.at[0])
    drain(rowtots.at[pl.ds(0, NR - 1)], rtsem.at[0])
    drain(sx.at[pl.ds(0, NX - 1)], ssem.at[0])
    drain(trows.at[pl.ds(0, NR - 1)], trsem.at[0])
    drain(prow.at[pl.ds(0, NR - 1)], psem.at[0])
    for k in range(NX - 1):
        drain(px.at[0], xsem.at[k, 0])
    drain(sqr.at[pl.ds(0, NHEAD - 1)], qsem.at[0])
    for j in range(G):
        three = kb.at[j, pl.ds(0, (NX - 1) * TOK)]
        drain(three, ksem.at[j, 0])

        @pl.when(r < NR - 1)
        def _():
            halo = kb.at[j, pl.ds(0, WIN)]
            drain(halo, khsem.at[j, 0])
            drain(halo, vhsem.at[j, 0])

        drain(three, aqsem.at[j, 0])
        drain(three, avsem.at[j, 0])
        if EARLY[j]:
            drain(three, losem.at[j, 0])


def body(lin_query, lin_key, lin_value, log_decay, soft_query, soft_key, soft_value):
    wide = (TOK, H * DH)
    vmem, dma = pltpu.VMEM, pltpu.SemaphoreType.DMA
    hbm = pl.BlockSpec(memory_space=pltpu.HBM)
    return pl.pallas_call(
        kernel,
        out_shape=[jax.ShapeDtypeStruct(wide, BF16)] * 2,
        in_specs=[hbm] * 3 + [pl.BlockSpec(memory_space=vmem)] + [hbm] * 3,
        out_specs=[hbm, hbm],
        scratch_shapes=[vmem(wide, BF16)] * 6
        + [
            vmem((H, TOK), F32),
            vmem((H, TOK, DH), F32),
            vmem((H, TOK, DH), F32),
            vmem((TOK, DH), F32),
            vmem((H, DH), F32),
            vmem((NX, H, DH), F32),
            vmem((H, 8, DH), F32),
            vmem((NR, 8, DH), F32),
            vmem((H, DH, DH), BF16),
            vmem((NX, G, DH, DH), BF16),
            vmem((NR, DH // 4, DH), BF16),
            vmem((NR, DH // 4, DH), BF16),
            vmem((NR, DH // 4, DH), BF16),
            vmem((NR, DH // 4, DH), BF16),
            vmem((NX, G, DH, DH), BF16),
            vmem((H, DH, DH), BF16),
            vmem((8, TOK), F32),
            vmem((NHEAD, 8, TOK), F32),
            vmem((G, SPAN, DH), BF16),
            vmem((G, SPAN, DH), BF16),
            vmem((G, LINE, DH), BF16),
            vmem((G, LINE, DH), BF16),
            vmem((G, LINE, DH), BF16),
            dma((9,)),
        ]
        + [dma((2,))] * 5
        + [dma((NX - 1, 2)), dma((2,))]
        + [dma((G, 2))] * 6
        + [dma((1,)), dma((1,))]
        + [pltpu.SemaphoreType.REGULAR] * 2,
        compiler_params=pltpu.CompilerParams(
            collective_id=1, has_side_effects=True, vmem_limit_bytes=60 * 2**20
        ),
        cost_estimate=pl.CostEstimate(
            flops=6 * 10**9, bytes_accessed=13 * 2**20, transcendentals=10**7
        ),
    )(lin_query, lin_key, lin_value, log_decay, soft_query, soft_key, soft_value)


def solution(mesh):
    spec = P("ctx", "head")
    return jax.shard_map(
        body,
        mesh=mesh,
        in_specs=(spec, spec, spec, P("head", "ctx"), spec, spec, spec),
        out_specs=(spec, spec),
        check_vma=False,
    )
```
